512 devices in a mesh: dp: 4 (over y), node: 16 (over z), local: 8 (over x, core).
Axes of the slice: x: 4, y: 4, z: 16, core: 2. Of those that a mesh axis runs over, the one named last changes fastest.
Arguments:
- tokens: bfloat16 [32768, 1024], P(('dp', 'node', 'local')), may hold values from -6 to 6
- upstream: bfloat16 [32768, 1024], P(('dp', 'node', 'local')), may hold values from -1.1953125 to 1.1953125
- expert_ids: int32 [32768, 4], P(('dp', 'node', 'local')), may hold values from 0 to 63, as said below
- gate_weights: bfloat16 [32768, 4], P(('dp', 'node', 'local')), may hold values from 0.099609375 to 1
- w_gate: bfloat16 [128, 352, 1024], P(('node', 'local')), may hold values from -0.1875 to 0.1875
- w_up: bfloat16 [128, 352, 1024], P(('node', 'local')), may hold values from -0.1875 to 0.1875
- w_down: bfloat16 [128, 352, 1024], P(('node', 'local')), may hold values from -0.21875 to 0.21875
Outputs:
- token_grads: bfloat16 [32768, 1024], P(('dp', 'node', 'local'))
- gate_grads: bfloat16 [128, 352, 1024], P(('node', 'local'), None, 'dp')
- up_grads: bfloat16 [128, 352, 1024], P(('node', 'local'), None, 'dp')
- down_grads: bfloat16 [128, 352, 1024], P(('node', 'local'), None, 'dp')
The draws below stay inside these ranges and needn't reach their ends.
Inputs may be any that keep to these rules, and one draw needn't show every extreme that they name: `expert_ids`: each row names 4 distinct experts, lying on exactly 3 distinct nodes, expert e lying on node e // 4. Of one device's 64 rows, exactly 12 name some expert on any given node, and at most 5 name any one expert; in every draw some experts are named by exactly 5 rows of every device.
All inputs are finite; a program needn't handle non-finite values.
Results may differ from the reference program's by a relative error of at most 0.013.
Values may be sent and summed in bfloat16 or wider, within the bound.
No kernel may reach another device: no remote copies, remote signals or barrier semaphores. Data moves between devices by JAX's collectives and lax.ppermute only.
A program may use at most 64 MiB of HBM per device.

```python
import math
import jax
import jax.numpy as jnp
from jax import lax

D = 1024
HIDDEN_SIZE = 704
TOK_DEV = 64
HALF = 352
GROUPS = 4
EXP_NODE = 4
EXPERTS = 64
NODE_LIMIT = 3
TOP = 4
TOKENS = 32768
CAP = 5
N_NODE = 16
N_LOCAL = 8
DEVICES = 512


def draw_expert_ids(key, part):
    key = jax.random.fold_in(key, 11)
    hot_key, block_key = jax.random.split(key)
    favoured = jax.random.randint(hot_key, (N_NODE,), 0, EXP_NODE).astype(jnp.int32)
    block_keys = jax.random.split(block_key, DEVICES)

    def one_block(this_key):
        order_key, node_key, shift_key = jax.random.split(this_key, 3)
        order = jax.random.permutation(order_key, TOK_DEV).astype(jnp.int32)
        others = jax.random.permutation(node_key, N_NODE - 1)[:NODE_LIMIT - 1].astype(jnp.int32) + 1
        offsets = jnp.concatenate([jnp.zeros((1,), jnp.int32), others], 0)
        shifts = jax.random.randint(shift_key, (NODE_LIMIT,), 0, EXP_NODE).astype(jnp.int32)
        home = order % N_NODE
        base_local = order // N_NODE % EXP_NODE
        nodes = (home[:, None] + offsets[None, :]) % N_NODE
        locals_here = (base_local[:, None] + shifts[None, :]) % EXP_NODE
        base = nodes * EXP_NODE + locals_here
        extra_nodes = nodes[:, :TOP - NODE_LIMIT]
        extra_base = locals_here[:, :TOP - NODE_LIMIT]
        hot_local = favoured[extra_nodes]
        drawn = (extra_base + 1) % EXP_NODE
        extra_local = jnp.where(extra_base == (hot_local + 1) % EXP_NODE, hot_local, drawn)
        extra = extra_nodes * EXP_NODE + extra_local
        return jnp.concatenate([base, extra], 1)
    return jax.vmap(one_block)(block_keys).reshape(TOK_DEV * DEVICES, TOP).astype(jnp.int32)


def steps_of(own_key, shape, shards, smallest, top_value):
    gain = 1.0
    for position, shards_of in shards:
        draws = jax.random.uniform(jax.random.fold_in(jax.random.fold_in(own_key, 6), position), (shards_of,), jnp.float32, smallest / len(shards), top_value / len(shards))
        gain = gain * jnp.repeat(jnp.exp(draws), shape[position] // shards_of).reshape((-1,) + (1,) * (len(shape) - 1 - position))
    return gain


def bell_draw(key, dims, width, bound, cuts=(), kind=jnp.bfloat16):
    values = jax.random.normal(key, dims, jnp.float32) * width
    if len(cuts) > 0:
        values = steps_of(key, dims, cuts, -0.22, 0.18) * values
    return jnp.clip(values, min=-bound, max=bound).astype(kind)


def setup_inputs(seed: int = 0) -> dict:
    key_list = jax.random.split(jax.random.key(seed), 8)
    return {
        "tokens": bell_draw(key_list[0], (TOKENS, D), 1.0, 6.0, ((0, 512),)),
        "upstream": bell_draw(key_list[1], (TOKENS, D), 0.2, 1.1953125, ((0, 512),)),
        "expert_ids": draw_expert_ids(jax.random.fold_in(key_list[7], 71), 0),
        "gate_weights": jnp.clip(jnp.exp(math.log(1.0) - 2.306499 * jax.random.uniform(key_list[3], (TOKENS, TOP), jnp.float32) ** steps_of(key_list[3], (TOKENS, TOP), ((0, 512),), -0.2, 0.2)), 0.099609375, 1.0).astype(jnp.bfloat16),
        "w_gate": bell_draw(key_list[4], (2 * EXPERTS, HALF, D), D ** -0.5, 0.1875, ((0, 128),)),
        "w_up": bell_draw(key_list[5], (2 * EXPERTS, HALF, D), D ** -0.5, 0.1875, ((0, 128),)),
        "w_down": bell_draw(key_list[6], (2 * EXPERTS, HALF, D), HIDDEN_SIZE ** -0.5, 0.21875, ((0, 128),)),
    }


contract_last = (((1,), (1,)), ((), ()))
contract_first = (((0,), (0,)), ((), ()))


def expert_backward(x_rows, cot_rows, gate_half, up_half, down_half):
    gate_logit = lax.dot_general(x_rows, gate_half, contract_last, preferred_element_type=jnp.float32)
    up_value = lax.dot_general(x_rows, up_half, contract_last, preferred_element_type=jnp.float32)
    gate_sigmoid = jax.nn.sigmoid(gate_logit)
    activation = gate_logit * gate_sigmoid
    hidden = (activation * up_value).astype(jnp.bfloat16)
    back_hidden = lax.dot_general(cot_rows, down_half, contract_last, preferred_element_type=jnp.float32)
    back_up = (back_hidden * activation).astype(jnp.bfloat16)
    back_gate = (back_hidden * up_value * gate_sigmoid * (1.0 + gate_logit * (1.0 - gate_sigmoid))).astype(jnp.bfloat16)
    partial_value = jnp.dot(back_gate, gate_half, preferred_element_type=jnp.float32) + jnp.dot(back_up, up_half, preferred_element_type=jnp.float32)
    grad_gate = lax.dot_general(back_gate, x_rows, contract_first, preferred_element_type=jnp.float32)
    grad_up = lax.dot_general(back_up, x_rows, contract_first, preferred_element_type=jnp.float32)
    grad_down = lax.dot_general(hidden, cot_rows, contract_first, preferred_element_type=jnp.float32)
    return partial_value.astype(jnp.bfloat16), grad_gate, grad_up, grad_down


def rounded(value):
    return lax.optimization_barrier(value.astype(jnp.bfloat16)).astype(jnp.float32)


def reference(tokens, upstream, expert_ids, gate_weights, w_gate, w_up, w_down):
    group_rows = TOKENS // GROUPS
    group_cap = CAP * N_NODE * N_LOCAL
    zero_row = jnp.zeros((1, D), jnp.bfloat16)

    def one_node(total, node):
        node_acc = jnp.zeros((TOKENS + 1, D), jnp.float32)
        node_grads = []
        for local in range(EXP_NODE):
            expert = node * EXP_NODE + local
            sums = [[jnp.zeros((HALF, D), jnp.float32) for kind in range(3)] for half in range(2)]
            for group in range(GROUPS):
                lower = group * group_rows
                ids_here = expert_ids[lower:lower + group_rows]
                match = ids_here == expert
                hit = jnp.any(match, axis=1)
                gate_here = jnp.sum(jnp.where(match, gate_weights[lower:lower + group_rows].astype(jnp.float32), 0.0), axis=1)
                picked = jnp.nonzero(hit, size=group_cap, fill_value=group_rows)[0].astype(jnp.int32)
                x_rows = jnp.concatenate([tokens[lower:lower + group_rows], zero_row], 0)[picked]
                dy_rows = jnp.concatenate([upstream[lower:lower + group_rows], zero_row], 0)[picked]
                gate_rows = jnp.concatenate([gate_here, jnp.zeros((1,), jnp.float32)], 0)[picked]
                cot_rows = (gate_rows[:, None] * dy_rows.astype(jnp.float32)).astype(jnp.bfloat16)
                pair_sum = jnp.zeros((group_cap, D), jnp.float32)
                for half in range(2):
                    index = 2 * expert + half
                    partial_value, grad_gate, grad_up, grad_down = expert_backward(x_rows, cot_rows, w_gate[index], w_up[index], w_down[index])
                    pair_sum = pair_sum + partial_value.astype(jnp.float32)
                    sums[half][0] = sums[half][0] + rounded(grad_gate)
                    sums[half][1] = sums[half][1] + rounded(grad_up)
                    sums[half][2] = sums[half][2] + rounded(grad_down)
                target = jnp.where(picked < group_rows, lower + picked, TOKENS).astype(jnp.int32)
                node_acc = node_acc.at[target].add(pair_sum)
            node_grads.append(sums[0])
            node_grads.append(sums[1])
        stacked = tuple(jnp.stack([item[kind] for item in node_grads], 0) for kind in range(3))
        return total + rounded(node_acc[:TOKENS]), stacked

    total, stacked = lax.scan(one_node, jnp.zeros((TOKENS, D), jnp.float32), jnp.arange(N_NODE, dtype=jnp.int32))
    gate_grads = stacked[0].reshape(2 * EXPERTS, HALF, D).astype(jnp.bfloat16)
    up_grads = stacked[1].reshape(2 * EXPERTS, HALF, D).astype(jnp.bfloat16)
    down_grads = stacked[2].reshape(2 * EXPERTS, HALF, D).astype(jnp.bfloat16)
    return (total.astype(jnp.bfloat16), gate_grads, up_grads, down_grads)
```

```python
import jax
import jax.numpy as jnp
from jax import lax
from jax.experimental import pallas as pl
from jax.experimental.pallas import tpu as pltpu
from jax.sharding import PartitionSpec as P

WIDTH = 1024
MID = 512
WIDE = 1536
META = 1664
HALF = 352
TOKS = 64
NODES = 16
MSG = 128
CAP = 5
SLOT = 80
SENT = 320
ROWS = 640
F32 = jnp.float32
BF = jnp.bfloat16
SAME_CORE = [[0, 2, 4, 6], [1, 3, 5, 7]]
OTHER_CORE = [(i, i ^ 1) for i in range(8)]


def mm(a, b):
    return jnp.dot(a, b, preferred_element_type=F32)


def mm_first(a, b):
    return lax.dot_general(a, b, (((0,), (0,)), ((), ())), preferred_element_type=F32)


def mm_last(a, b):
    return lax.dot_general(a, b, (((1,), (1,)), ((), ())), preferred_element_type=F32)


def iota(shape, dim):
    return lax.broadcasted_iota(jnp.int32, shape, dim)


def one(cond):
    return jnp.where(cond, 1.0, 0.0).astype(BF)


def route_body(tok_ref, up_ref, ids_ref, gate_ref, xmsg_ref, umsg_ref, sel_ref):
    ids = ids_ref[...]
    gates = gate_ref[...].astype(F32)
    lane_node = iota((TOKS, MSG), 1) >> 3
    lane_expert = iota((TOKS, TOKS), 1)
    named = jnp.zeros((TOKS, MSG), F32)
    weight = jnp.zeros((TOKS, TOKS), F32)
    for k in range(4):
        column = ids[:, k : k + 1]
        named = jnp.where((column >> 2) == lane_node, 1.0, named)
        weight = jnp.where(column == lane_expert, gates[:, k : k + 1], weight)
    named = named.astype(BF)
    weight = weight.astype(BF)
    row, col = iota((TOKS, TOKS), 0), iota((TOKS, TOKS), 1)
    hit = mm_first(named, one(row == col)) > 0.5
    rank = mm_first(named, one(row < col)).astype(jnp.int32)
    place = iota((MSG, TOKS), 0) & 7
    late = hit & (rank == 8 + (place & 3))
    whole = one(hit & (rank == place))
    left = one(late & (place < 4))
    right = one(late & (place >= 4))
    sel_ref[0] = whole
    sel_ref[1] = left
    sel_ref[2] = right
    for src, dst in ((tok_ref, xmsg_ref), (up_ref, umsg_ref)):
        dst[:, :WIDTH] = mm(whole, src[...]).astype(BF)
        dst[:, WIDTH:WIDE] = (mm(left, src[:, :MID]) + mm(right, src[:, MID:])).astype(BF)
    own_node = (iota((MSG, TOKS), 1) >> 2) == (iota((MSG, TOKS), 0) >> 3)
    gate_whole = jnp.where(own_node, mm(whole, weight), 0.0).astype(BF)
    gate_late = jnp.where(own_node, mm(left + right, weight), 0.0).astype(BF)
    fold_row, fold_col = iota((TOKS, MSG), 0) & 3, iota((TOKS, MSG), 1)
    meta = mm(gate_whole, one(fold_col == fold_row)) + mm(gate_late, one(fold_col == fold_row + 8))
    xmsg_ref[:, WIDE:] = meta.astype(BF)


def spread(sel, msg_ref, out_ref):
    low = msg_ref[:, WIDTH:WIDE]
    out_ref[:, :MID] = (mm(sel[:, :MSG], msg_ref[:, :MID]) + mm(sel[:, MSG : 2 * MSG], low)).astype(BF)
    out_ref[:, MID:] = (mm(sel[:, :MSG], msg_ref[:, MID:WIDTH]) + mm(sel[:, 2 * MSG :], low)).astype(BF)


def place_body(msg_ref, out_ref, sel_ref, gated_ref):
    row, col = iota((MSG, MSG), 0), iota((MSG, MSG), 1)
    gates = mm_first(msg_ref[:, WIDE:], one(row == col))
    gate_whole, gate_late = gates[0:8], gates[8:16]
    has_whole, has_late = one(gate_whole > 0.0), one(gate_late > 0.0)
    same = (row >> 3) == (col >> 3)
    rank_whole = mm(has_whole, one(same & (row < col)))
    rank_late = mm(has_whole, one(same)) + mm(has_late, one(same & ((row & 7) < (col & 3))))
    node = (iota((8, MSG), 1) >> 3) * CAP
    lane_place = iota((8, MSG), 1) & 7
    slot_whole = jnp.where(gate_whole > 0.0, node + rank_whole.astype(jnp.int32), -1)
    slot_late = jnp.where(gate_late > 0.0, node + rank_late.astype(jnp.int32), -1)
    slot_left = jnp.where(lane_place < 4, slot_late, -1)
    slot_right = jnp.where(lane_place >= 4, slot_late, -1)
    slots = iota((SLOT, MSG), 0)
    for j in range(4):
        parts = ((slot_whole, gate_whole), (slot_left, gate_late), (slot_right, gate_late))
        for part, (slot, gate) in enumerate(parts):
            match = slots == slot[j : j + 1]
            rows, lanes = pl.ds(j * SLOT, SLOT), pl.ds(part * MSG, MSG)
            sel_ref[rows, lanes] = one(match)
            gated_ref[rows, lanes] = jnp.where(match, gate[j : j + 1], 0.0).astype(BF)
    spread(sel_ref, msg_ref, out_ref)


def cotangent_body(msg_ref, gated_ref, out_ref):
    spread(gated_ref, msg_ref, out_ref)


def forward_body(own_ref, rest_ref, gate_ref, up_ref, act_ref, slope_ref, hidden_ref):
    for source, base in ((own_ref, 0), (rest_ref, SENT)):
        for start in range(0, SENT, 160):
            rows = source[start : start + 160]
            out = pl.ds(base + start, 160)
            gate_logit = mm_last(rows, gate_ref[...])
            up_value = mm_last(rows, up_ref[...])
            sig = jax.nn.sigmoid(gate_logit)
            act = gate_logit * sig
            act_ref[out] = act
            hidden_ref[out] = (act * up_value).astype(BF)
            slope_ref[out] = up_value * sig * (1.0 + gate_logit * (1.0 - sig))


def backward_body(own_ref, rest_ref, down_ref, gate_ref, up_ref, act_ref, slope_ref, piece_own, piece_rest, bg_ref, bu_ref):
    for source, target, base in ((rest_ref, piece_rest, SENT), (own_ref, piece_own, 0)):
        for start in range(0, SENT, 160):
            out = pl.ds(base + start, 160)
            back_hidden = mm_last(source[start : start + 160], down_ref[...])
            back_up = (back_hidden * act_ref[out]).astype(BF)
            back_gate = (back_hidden * slope_ref[out]).astype(BF)
            bg_ref[out] = back_gate
            bu_ref[out] = back_up
            target[start : start + 160] = (mm(back_gate, gate_ref[...]) + mm(back_up, up_ref[...])).astype(BF)


def grads_body(x_own, x_rest, c_own, c_rest, bg_ref, bu_ref, hidden_ref, out_ref):
    parts = ((bg_ref, x_own, x_rest), (bu_ref, x_own, x_rest), (hidden_ref, c_own, c_rest))
    for kind, (lhs, own, rest) in enumerate(parts):
        total = mm_first(lhs[:SENT], own[...]) + mm_first(lhs[SENT:], rest[...])
        for d in range(4):
            out_ref[d, kind * HALF : (kind + 1) * HALF] = total[:, d * 256 : (d + 1) * 256].astype(BF)


def combine_body(own_ref, other_ref, out_slots):
    out_slots[...] = (own_ref[...].astype(F32) + other_ref[...].astype(F32)).astype(BF)


def node_body(sel_ref, ret_ref, out_ref):
    out_ref[:, :WIDTH] = mm_first(sel_ref[:, :MSG], ret_ref[...]).astype(BF)
    out_ref[:, WIDTH:] = (
        mm_first(sel_ref[:, MSG : 2 * MSG], ret_ref[:, :MID])
        + mm_first(sel_ref[:, 2 * MSG :], ret_ref[:, MID:])
    ).astype(BF)


def final_body(sel_ref, msg_ref, out_ref):
    low = msg_ref[:, WIDTH:]
    out_ref[:, :MID] = (mm_first(sel_ref[0], msg_ref[:, :MID]) + mm_first(sel_ref[1], low)).astype(BF)
    out_ref[:, MID:] = (mm_first(sel_ref[0], msg_ref[:, MID:WIDTH]) + mm_first(sel_ref[2], low)).astype(BF)


def call(body, outs, flops, moved, *args):
    shapes = tuple(jax.ShapeDtypeStruct(s, t) for s, t in outs)
    whole = pl.BlockSpec(memory_space=pltpu.VMEM)
    return pl.pallas_call(
        body,
        out_shape=shapes,
        in_specs=[whole] * len(args),
        out_specs=tuple([whole] * len(outs)),
        compiler_params=pltpu.CompilerParams(vmem_limit_bytes=32 * 1024 * 1024),
        cost_estimate=pl.CostEstimate(flops=flops, bytes_accessed=moved, transcendentals=0),
        name=body.__name__,
    )(*args)


def over_nodes(x):
    return lax.all_to_all(x, "node", split_axis=0, concat_axis=0, tiled=True)


def over_chips(x):
    return lax.all_to_all(x, "local", split_axis=0, concat_axis=0, tiled=True, axis_index_groups=SAME_CORE)


def other_core(x):
    return lax.ppermute(x, "local", OTHER_CORE)


def on_device(tokens, upstream, expert_ids, gate_weights, w_gate, w_up, w_down):
    gate_half, up_half, down_half = w_gate[0], w_up[0], w_down[0]
    xmsg, umsg, row_sel = call(
        route_body,
        [((MSG, META), BF), ((MSG, WIDE), BF), ((3, MSG, TOKS), BF)],
        60_000_000,
        1_300_000,
        tokens,
        upstream,
        expert_ids,
        gate_weights,
    )
    x_in = over_nodes(xmsg)
    u_in = over_nodes(umsg)
    x_out, slot_sel, slot_gated = call(
        place_body,
        [((SENT, WIDTH), BF), ((SENT, 3 * MSG), BF), ((SENT, 3 * MSG), BF)],
        200_000_000,
        1_500_000,
        x_in,
    )
    x_own = over_chips(x_out)
    x_rest = other_core(x_own)
    act, slope, hidden = call(
        forward_body,
        [((ROWS, HALF), F32), ((ROWS, HALF), F32), ((ROWS, HALF), BF)],
        920_000_000,
        6_000_000,
        x_own,
        x_rest,
        gate_half,
        up_half,
    )
    (c_out,) = call(cotangent_body, [((SENT, WIDTH), BF)], 200_000_000, 1_300_000, u_in, slot_gated)
    c_own = over_chips(c_out)
    c_rest = other_core(c_own)
    piece_own, piece_rest, back_gate, back_up = call(
        backward_body,
        [((SENT, WIDTH), BF), ((SENT, WIDTH), BF), ((ROWS, HALF), BF), ((ROWS, HALF), BF)],
        1_400_000_000,
        8_000_000,
        c_own,
        c_rest,
        down_half,
        gate_half,
        up_half,
        act,
        slope,
    )
    piece_other = other_core(piece_rest)
    (grads,) = call(
        grads_body,
        [((4, 3 * HALF, 256), BF)],
        1_400_000_000,
        7_000_000,
        x_own,
        x_rest,
        c_own,
        c_rest,
        back_gate,
        back_up,
        hidden,
    )
    summed = lax.psum_scatter(grads.reshape(12 * HALF, 256), "dp", scatter_dimension=0, tiled=True)
    (pair_sum,) = call(combine_body, [((SENT, WIDTH), BF)], 1_000_000, 2_000_000, piece_own, piece_other)
    returned = over_chips(pair_sum)
    (node_sum,) = call(node_body, [((MSG, WIDE), BF)], 200_000_000, 1_300_000, slot_sel, returned)
    node_back = over_nodes(node_sum)
    (token_grads,) = call(final_body, [((TOKS, WIDTH), BF)], 50_000_000, 600_000, row_sel, node_back)
    return (
        token_grads,
        summed[None, :HALF],
        summed[None, HALF : 2 * HALF],
        summed[None, 2 * HALF :],
    )


def solution(mesh):
    tok = P(("dp", "node", "local"), None)
    weight = P(("node", "local"), None, None)
    grad = P(("node", "local"), None, "dp")
    return jax.shard_map(
        on_device,
        mesh=mesh,
        in_specs=(tok, tok, tok, tok, weight, weight, weight),
        out_specs=(tok, grad, grad, grad),
        check_vma=False,
    )
```

```python
import jax
import jax.numpy as jnp
from jax import lax
from jax.experimental import pallas as pl
from jax.experimental.pallas import tpu as pltpu
from jax.sharding import PartitionSpec as P

WIDTH = 1024
MID = 512
WIDE = 1536
META = 3072
HALF = 352
TOKS = 64
MSG = 128
CAP = 5
SLOT = 80
SENT = 320
F32 = jnp.float32
BF = jnp.bfloat16
SAME_CORE = [[0, 2, 4, 6], [1, 3, 5, 7]]
OTHER_CORE = [(i, i ^ 1) for i in range(8)]
VMEM = pl.BlockSpec(memory_space=pltpu.VMEM)
HBM = pl.BlockSpec(memory_space=pltpu.HBM)


def mm(a, b):
    return jnp.dot(a, b, preferred_element_type=F32)


def mm_first(a, b):
    return lax.dot_general(a, b, (((0,), (0,)), ((), ())), preferred_element_type=F32)


def mm_last(a, b):
    return lax.dot_general(a, b, (((1,), (1,)), ((), ())), preferred_element_type=F32)


def iota(shape, dim):
    return lax.broadcasted_iota(jnp.int32, shape, dim)


def one(cond):
    return jnp.where(cond, 1.0, 0.0).astype(BF)


def route_body(ids_hbm, gate_hbm, tok_hbm, up_hbm, msg_ref, sel_hbm, ids_ref, gate_ref, tok_ref, up_ref, sel_ref, sems):
    pairs = ((ids_hbm, ids_ref), (gate_hbm, gate_ref), (tok_hbm, tok_ref), (up_hbm, up_ref))
    loads = [pltpu.make_async_copy(src, dst, sems.at[i]) for i, (src, dst) in enumerate(pairs)]
    for load in loads:
        load.start()
    loads[0].wait()
    loads[1].wait()
    ids = ids_ref[...]
    gates = gate_ref[...].astype(F32)
    node = iota((MSG, TOKS), 0) >> 3
    expert = iota((TOKS, TOKS), 0)
    named = jnp.zeros((MSG, TOKS), F32)
    weight = jnp.zeros((TOKS, TOKS), F32)
    for k in range(4):
        row = ids[k : k + 1]
        named = jnp.where((row >> 2) == node, 1.0, named)
        weight = jnp.where(row == expert, gates[k : k + 1], weight)
    weight = weight.astype(BF)
    hit = named > 0.5
    rank = mm(named.astype(BF), one(iota((TOKS, TOKS), 0) < iota((TOKS, TOKS), 1))).astype(jnp.int32)
    place = iota((MSG, TOKS), 0) & 7
    late = hit & (rank == 8 + (place & 3))
    whole = one(hit & (rank == place))
    left = one(late & (place < 4))
    right = one(late & (place >= 4))
    sel_ref[0] = whole
    sel_ref[1] = left
    sel_ref[2] = right
    store = pltpu.make_async_copy(sel_ref, sel_hbm, sems.at[4])
    store.start()
    own_node = (iota((MSG, TOKS), 1) >> 2) == node
    gate_whole = jnp.where(own_node, mm_last(whole, weight), 0.0).astype(BF)
    gate_late = jnp.where(own_node, mm_last(left + right, weight), 0.0).astype(BF)
    fold_row, fold_col = iota((TOKS, MSG), 0) & 3, iota((TOKS, MSG), 1)
    meta = mm(gate_whole, one(fold_col == fold_row)) + mm(gate_late, one(fold_col == fold_row + 8))
    msg_ref[:, META:] = meta.astype(BF)
    for load, src, base in ((loads[2], tok_ref, 0), (loads[3], up_ref, WIDE)):
        load.wait()
        msg_ref[:, base : base + WIDTH] = mm(whole, src[...]).astype(BF)
        low = mm(left, src[:, :MID]) + mm(right, src[:, MID:])
        msg_ref[:, base + WIDTH : base + WIDE] = low.astype(BF)
    store.wait()


def spread(sel, msg_ref, at, out_ref, to):
    low = msg_ref[:, at + WIDTH : at + WIDE]
    left = mm(sel[:, :MSG], msg_ref[:, at : at + MID]) + mm(sel[:, MSG : 2 * MSG], low)
    right = mm(sel[:, :MSG], msg_ref[:, at + MID : at + WIDTH]) + mm(sel[:, 2 * MSG :], low)
    out_ref[:, to : to + MID] = left.astype(BF)
    out_ref[:, to + MID : to + WIDTH] = right.astype(BF)


def place_body(msg_ref, out_ref, sel_hbm, sel_ref, gated_ref, sem):
    row, col = iota((MSG, MSG), 0), iota((MSG, MSG), 1)
    gates = mm_first(msg_ref[:, META:], one(row == col))
    gate_whole, gate_late = gates[0:8], gates[8:16]
    has_whole, has_late = one(gate_whole > 0.0), one(gate_late > 0.0)
    same = (row >> 3) == (col >> 3)
    rank_whole = mm(has_whole, one(same & (row < col)))
    rank_late = mm(has_whole, one(same)) + mm(has_late, one(same & ((row & 7) < (col & 3))))
    node = (iota((8, MSG), 1) >> 3) * CAP
    lane_place = iota((8, MSG), 1) & 7
    slot_whole = jnp.where(gate_whole > 0.0, node + rank_whole.astype(jnp.int32), -1)
    slot_late = jnp.where(gate_late > 0.0, node + rank_late.astype(jnp.int32), -1)
    slot_left = jnp.where(lane_place < 4, slot_late, -1)
    slot_right = jnp.where(lane_place >= 4, slot_late, -1)
    slots = iota((SLOT, MSG), 0)
    for j in range(4):
        parts = ((slot_whole, gate_whole), (slot_left, gate_late), (slot_right, gate_late))
        for part, (slot, gate) in enumerate(parts):
            match = slots == slot[j : j + 1]
            rows, lanes = pl.ds(j * SLOT, SLOT), pl.ds(part * MSG, MSG)
            sel_ref[rows, lanes] = one(match)
            gated_ref[rows, lanes] = jnp.where(match, gate[j : j + 1], 0.0).astype(BF)
    store = pltpu.make_async_copy(sel_ref, sel_hbm, sem)
    store.start()
    spread(sel_ref, msg_ref, 0, out_ref, 0)
    spread(gated_ref, msg_ref, WIDE, out_ref, WIDTH)
    store.wait()


def activate(x, gate_ref, up_ref):
    gate_logit = mm_last(x, gate_ref[...])
    up_value = mm_last(x, up_ref[...])
    sig = jax.nn.sigmoid(gate_logit)
    act = gate_logit * sig
    return act, up_value * sig * (1.0 + gate_logit * (1.0 - sig)), (act * up_value).astype(BF)


def own_body(*refs):
    hbm, (piece_hbm, bg_hbm, bu_hbm, hidden_hbm) = refs[0:7], refs[7:11]
    vmem, (total_ref, piece_ref, bg_ref, bu_ref, hidden_ref, sems) = refs[11:18], refs[18:]
    loads = [pltpu.make_async_copy(src, dst, sems.at[i]) for i, (src, dst) in enumerate(zip(hbm, vmem))]
    for load in loads:
        load.start()
    backs = ((bg_ref, bg_hbm), (bu_ref, bu_hbm), (hidden_ref, hidden_hbm))
    stores = [pltpu.make_async_copy(src, dst, sems.at[7 + i]) for i, (src, dst) in enumerate(backs)]
    xc_ref = vmem[0]
    loads[0].wait()
    for half in range(2):
        gate_ref, up_ref, down_ref = vmem[1 + 3 * half : 4 + 3 * half]
        for load in loads[1 + 3 * half : 4 + 3 * half]:
            load.wait()
        for start in range(0, SENT, 160):
            rows = pl.ds(start, 160)
            x, c = xc_ref[rows, :WIDTH], xc_ref[rows, WIDTH:]
            act, slope, hidden = activate(x, gate_ref, up_ref)
            back_hidden = mm_last(c, down_ref[...])
            back_up = (back_hidden * act).astype(BF)
            back_gate = (back_hidden * slope).astype(BF)
            part = mm(back_gate, gate_ref[...]) + mm(back_up, up_ref[...])
            if half == 0:
                bg_ref[rows] = back_gate
                bu_ref[rows] = back_up
                hidden_ref[rows] = hidden
                total_ref[rows] = part
            else:
                piece_ref[rows] = (total_ref[rows] + part).astype(BF)
        if half == 0:
            for store in stores:
                store.start()
    last = pltpu.make_async_copy(piece_ref, piece_hbm, sems.at[10])
    last.start()
    for store in stores:
        store.wait()
    last.wait()


def grads_body(*refs):
    hbm, out_hbm, vmem, (out_ref, bg2_ref, bu2_ref, hidden2_ref, sems) = refs[0:8], refs[8], refs[9:17], refs[17:]
    loads = [pltpu.make_async_copy(src, dst, sems.at[i]) for i, (src, dst) in enumerate(zip(hbm, vmem))]
    for load in loads:
        load.start()
    rest_ref, gate_ref, up_ref, down_ref, own_ref, bg_ref, bu_ref, hidden_ref = vmem
    for load in loads[:4]:
        load.wait()
    for start in range(0, SENT, 160):
        rows = pl.ds(start, 160)
        act, slope, hidden2_ref[rows] = activate(rest_ref[rows, :WIDTH], gate_ref, up_ref)
        back_hidden = mm_last(rest_ref[rows, WIDTH:], down_ref[...])
        bu2_ref[rows] = (back_hidden * act).astype(BF)
        bg2_ref[rows] = (back_hidden * slope).astype(BF)
    for load in loads[4:]:
        load.wait()
    parts = ((bg_ref, bg2_ref, 0), (bu_ref, bu2_ref, 0), (hidden_ref, hidden2_ref, WIDTH))
    stores = []
    for kind, (lhs_own, lhs_rest, at) in enumerate(parts):
        cols = pl.ds(at, WIDTH)
        total = mm_first(lhs_own[...], own_ref[:, cols]) + mm_first(lhs_rest[...], rest_ref[:, cols])
        rows = pl.ds(kind * HALF, HALF)
        for d in range(4):
            out_ref[d, rows] = total[:, d * 256 : (d + 1) * 256].astype(BF)
        stores.append(pltpu.make_async_copy(out_ref.at[:, rows], out_hbm.at[:, rows], sems.at[8 + kind]))
        stores[-1].start()
    for store in stores:
        store.wait()


def node_body(sel_ref, ret_ref, out_ref):
    out_ref[:, :WIDTH] = mm_first(sel_ref[:, :MSG], ret_ref[...]).astype(BF)
    out_ref[:, WIDTH:] = (
        mm_first(sel_ref[:, MSG : 2 * MSG], ret_ref[:, :MID])
        + mm_first(sel_ref[:, 2 * MSG :], ret_ref[:, MID:])
    ).astype(BF)


def final_body(sum_hbm, sel_hbm, msg_hbm, out_hbm, gate_hbm, up_hbm, down_hbm, sum_ref, sel_ref, msg_ref, out_ref, sems):
    grads = []
    for kind, grad_hbm in enumerate((gate_hbm, up_hbm, down_hbm)):
        part = pl.ds(kind * HALF, HALF)
        load = pltpu.make_async_copy(sum_hbm.at[part], sum_ref.at[part], sems.at[kind])
        grads.append((load, pltpu.make_async_copy(sum_ref.at[part], grad_hbm, sems.at[3 + kind])))
    loads = [pltpu.make_async_copy(sel_hbm, sel_ref, sems.at[6]), pltpu.make_async_copy(msg_hbm, msg_ref, sems.at[7])]
    for load in loads:
        load.start()
    for load, _ in grads:
        load.start()
    for load, store in grads:
        load.wait()
        store.start()
    for load in loads:
        load.wait()
    low = msg_ref[:, WIDTH:]
    out_ref[:, :MID] = (mm_first(sel_ref[0], msg_ref[:, :MID]) + mm_first(sel_ref[1], low)).astype(BF)
    out_ref[:, MID:] = (mm_first(sel_ref[0], msg_ref[:, MID:WIDTH]) + mm_first(sel_ref[2], low)).astype(BF)
    last = pltpu.make_async_copy(out_ref, out_hbm, sems.at[8])
    last.start()
    for _, store in grads:
        store.wait()
    last.wait()


def call(body, ins, outs, flops, moved, *args, scratch=(), limit=60):
    return pl.pallas_call(
        body,
        out_shape=tuple(jax.ShapeDtypeStruct(s, BF) for s, _ in outs),
        in_specs=list(ins),
        out_specs=tuple(m for _, m in outs),
        scratch_shapes=list(scratch),
        compiler_params=pltpu.CompilerParams(vmem_limit_bytes=limit * 1024 * 1024),
        cost_estimate=pl.CostEstimate(flops=flops, bytes_accessed=moved, transcendentals=0),
        name=body.__name__,
    )(*args)


def over_nodes(x):
    return lax.all_to_all(x, "node", split_axis=0, concat_axis=0, tiled=True)


def over_chips(x):
    return lax.all_to_all(x, "local", split_axis=0, concat_axis=0, tiled=True, axis_index_groups=SAME_CORE)


def other_core(x):
    return lax.ppermute(x, "local", OTHER_CORE)


def on_device(tokens, upstream, expert_ids, gate_weights, w_gate, w_up, w_down):
    own = (w_gate[0], w_up[0], w_down[0])
    message, row_sel = call(
        route_body,
        [HBM] * 4,
        [((MSG, META + 128), VMEM), ((3, MSG, TOKS), HBM)],
        80_000_000,
        1_300_000,
        expert_ids.T,
        gate_weights.T,
        tokens,
        upstream,
        scratch=[
            pltpu.VMEM((4, TOKS), jnp.int32),
            pltpu.VMEM((4, TOKS), BF),
            pltpu.VMEM((TOKS, WIDTH), BF),
            pltpu.VMEM((TOKS, WIDTH), BF),
            pltpu.VMEM((3, MSG, TOKS), BF),
            pltpu.SemaphoreType.DMA((5,)),
        ],
    )
    message, *sent = lax.optimization_barrier((message, *own))
    arrived, *rest = lax.optimization_barrier((over_nodes(message), *(other_core(w) for w in sent)))
    placed, slot_sel = call(
        place_body,
        [VMEM],
        [((SENT, 2 * WIDTH), VMEM), ((SENT, 3 * MSG), HBM)],
        400_000_000,
        2_300_000,
        arrived,
        scratch=[pltpu.VMEM((SENT, 3 * MSG), BF), pltpu.VMEM((SENT, 3 * MSG), BF), pltpu.SemaphoreType.DMA],
        limit=16,
    )
    rows_own = over_chips(placed)
    rows_rest = other_core(rows_own)
    piece, *back_own = call(
        own_body,
        [HBM] * 7,
        [((SENT, WIDTH), HBM)] + [((SENT, HALF), HBM)] * 3,
        2_300_000_000,
        7_000_000,
        rows_own,
        *own,
        *rest,
        scratch=[
            pltpu.VMEM((SENT, 2 * WIDTH), BF),
            *[pltpu.VMEM((HALF, WIDTH), BF)] * 6,
            pltpu.VMEM((SENT, WIDTH), F32),
            pltpu.VMEM((SENT, WIDTH), BF),
            *[pltpu.VMEM((SENT, HALF), BF)] * 3,
            pltpu.SemaphoreType.DMA((11,)),
        ],
    )
    returned = over_chips(piece)
    (grads,) = call(
        grads_body,
        [HBM] * 8,
        [((4, 3 * HALF, 256), HBM)],
        2_100_000_000,
        8_000_000,
        rows_rest,
        *own,
        rows_own,
        *back_own,
        scratch=[
            pltpu.VMEM((SENT, 2 * WIDTH), BF),
            *[pltpu.VMEM((HALF, WIDTH), BF)] * 3,
            pltpu.VMEM((SENT, 2 * WIDTH), BF),
            *[pltpu.VMEM((SENT, HALF), BF)] * 3,
            pltpu.VMEM((4, 3 * HALF, 256), BF),
            *[pltpu.VMEM((SENT, HALF), BF)] * 3,
            pltpu.SemaphoreType.DMA((11,)),
        ],
    )
    summed = lax.psum_scatter(grads.reshape(12 * HALF, 256), "dp", scatter_dimension=0, tiled=True)
    (node_sum,) = call(node_body, [VMEM] * 2, [((MSG, WIDE), VMEM)], 50_000_000_000, 1_300_000, slot_sel, returned, limit=16)
    token_grads, *weight_grads = call(
        final_body,
        [HBM] * 3,
        [((TOKS, WIDTH), HBM)] + [((HALF, 256), HBM)] * 3,
        50_000_000,
        1_600_000,
        summed,
        row_sel,
        over_nodes(node_sum),
        scratch=[
            pltpu.VMEM((3 * HALF, 256), BF),
            pltpu.VMEM((3, MSG, TOKS), BF),
            pltpu.VMEM((MSG, WIDE), BF),
            pltpu.VMEM((TOKS, WIDTH), BF),
            pltpu.SemaphoreType.DMA((9,)),
        ],
    )
    return (token_grads, *[g[None] for g in weight_grads])


def solution(mesh):
    tok = P(("dp", "node", "local"), None)
    weight = P(("node", "local"), None, None)
    grad = P(("node", "local"), None, "dp")
    return jax.shard_map(
        on_device,
        mesh=mesh,
        in_specs=(tok, tok, tok, tok, weight, weight, weight),
        out_specs=(tok, grad, grad, grad),
        check_vma=False,
    )
```

```python
import jax
import jax.numpy as jnp
from jax import lax
from jax.experimental import pallas as pl
from jax.experimental.pallas import tpu as pltpu
from jax.sharding import PartitionSpec as P

WIDTH = 1024
MID = 512
WIDE = 1536
META = 3072
HALF = 352
TOKS = 64
MSG = 128
CAP = 5
SLOT = 80
SENT = 320
F32 = jnp.float32
BF = jnp.bfloat16
SAME_CORE = [[0, 2, 4, 6], [1, 3, 5, 7]]
OTHER_CORE = [(i, i ^ 1) for i in range(8)]
VMEM = pl.BlockSpec(memory_space=pltpu.VMEM)
HBM = pl.BlockSpec(memory_space=pltpu.HBM)


def mm(a, b):
    return jnp.dot(a, b, preferred_element_type=F32)


def mm_first(a, b):
    return lax.dot_general(a, b, (((0,), (0,)), ((), ())), preferred_element_type=F32)


def mm_last(a, b):
    return lax.dot_general(a, b, (((1,), (1,)), ((), ())), preferred_element_type=F32)


def iota(shape, dim):
    return lax.broadcasted_iota(jnp.int32, shape, dim)


def one(cond):
    return jnp.where(cond, 1.0, 0.0).astype(BF)


def route_body(ids_hbm, gate_hbm, tok_hbm, up_hbm, msg_ref, sel_hbm, ids_ref, gate_ref, tok_ref, up_ref, sel_ref, sems):
    pairs = ((ids_hbm, ids_ref), (gate_hbm, gate_ref), (tok_hbm, tok_ref), (up_hbm, up_ref))
    loads = [pltpu.make_async_copy(src, dst, sems.at[i]) for i, (src, dst) in enumerate(pairs)]
    for load in loads:
        load.start()
    loads[0].wait()
    loads[1].wait()
    ids = ids_ref[...]
    gates = gate_ref[...].astype(F32)
    node = iota((MSG, TOKS), 0) >> 3
    expert = iota((TOKS, TOKS), 0)
    named = jnp.zeros((MSG, TOKS), F32)
    weight = jnp.zeros((TOKS, TOKS), F32)
    for k in range(4):
        row = ids[k : k + 1]
        named = jnp.where((row >> 2) == node, 1.0, named)
        weight = jnp.where(row == expert, gates[k : k + 1], weight)
    weight = weight.astype(BF)
    hit = named > 0.5
    rank = mm(named.astype(BF), one(iota((TOKS, TOKS), 0) < iota((TOKS, TOKS), 1))).astype(jnp.int32)
    place = iota((MSG, TOKS), 0) & 7
    late = hit & (rank == 8 + (place & 3))
    whole = one(hit & (rank == place))
    left = one(late & (place < 4))
    right = one(late & (place >= 4))
    sel_ref[0] = whole
    sel_ref[1] = left
    sel_ref[2] = right
    store = pltpu.make_async_copy(sel_ref, sel_hbm, sems.at[4])
    store.start()
    own_node = (iota((MSG, TOKS), 1) >> 2) == node
    gate_whole = jnp.where(own_node, mm_last(whole, weight), 0.0).astype(BF)
    gate_late = jnp.where(own_node, mm_last(left + right, weight), 0.0).astype(BF)
    fold_row, fold_col = iota((TOKS, MSG), 0) & 3, iota((TOKS, MSG), 1)
    meta = mm(gate_whole, one(fold_col == fold_row)) + mm(gate_late, one(fold_col == fold_row + 8))
    msg_ref[:, META:] = meta.astype(BF)
    for load, src, base in ((loads[2], tok_ref, 0), (loads[3], up_ref, WIDE)):
        load.wait()
        msg_ref[:, base : base + WIDTH] = mm(whole, src[...]).astype(BF)
        low = mm(left, src[:, :MID]) + mm(right, src[:, MID:])
        msg_ref[:, base + WIDTH : base + WIDE] = low.astype(BF)
    store.wait()


def spread(sel, msg_ref, at, out_ref, to):
    low = msg_ref[:, at + WIDTH : at + WIDE]
    left = mm(sel[:, :MSG], msg_ref[:, at : at + MID]) + mm(sel[:, MSG : 2 * MSG], low)
    right = mm(sel[:, :MSG], msg_ref[:, at + MID : at + WIDTH]) + mm(sel[:, 2 * MSG :], low)
    out_ref[:, to : to + MID] = left.astype(BF)
    out_ref[:, to + MID : to + WIDTH] = right.astype(BF)


def place_body(msg_ref, out_ref, sel_hbm, sel_ref, gated_ref, sem):
    row, col = iota((MSG, MSG), 0), iota((MSG, MSG), 1)
    gates = mm_first(msg_ref[:, META:], one(row == col))
    gate_whole, gate_late = gates[0:8], gates[8:16]
    has_whole, has_late = one(gate_whole > 0.0), one(gate_late > 0.0)
    same = (row >> 3) == (col >> 3)
    rank_whole = mm(has_whole, one(same & (row < col)))
    rank_late = mm(has_whole, one(same)) + mm(has_late, one(same & ((row & 7) < (col & 3))))
    node = (iota((8, MSG), 1) >> 3) * CAP
    lane_place = iota((8, MSG), 1) & 7
    slot_whole = jnp.where(gate_whole > 0.0, node + rank_whole.astype(jnp.int32), -1)
    slot_late = jnp.where(gate_late > 0.0, node + rank_late.astype(jnp.int32), -1)
    slot_left = jnp.where(lane_place < 4, slot_late, -1)
    slot_right = jnp.where(lane_place >= 4, slot_late, -1)
    slots = iota((SLOT, MSG), 0)
    for j in range(4):
        parts = ((slot_whole, gate_whole), (slot_left, gate_late), (slot_right, gate_late))
        for part, (slot, gate) in enumerate(parts):
            match = slots == slot[j : j + 1]
            rows, lanes = pl.ds(j * SLOT, SLOT), pl.ds(part * MSG, MSG)
            sel_ref[rows, lanes] = one(match)
            gated_ref[rows, lanes] = jnp.where(match, gate[j : j + 1], 0.0).astype(BF)
    store = pltpu.make_async_copy(sel_ref, sel_hbm, sem)
    store.start()
    spread(sel_ref, msg_ref, 0, out_ref, 0)
    spread(gated_ref, msg_ref, WIDE, out_ref, WIDTH)
    store.wait()


def activate(x, gate_ref, up_ref):
    gate_logit = mm_last(x, gate_ref[...])
    up_value = mm_last(x, up_ref[...])
    sig = jax.nn.sigmoid(gate_logit)
    act = gate_logit * sig
    return act, up_value * sig * (1.0 + gate_logit * (1.0 - sig)), (act * up_value).astype(BF)


def own_body(xc_ref, *refs):
    own, rest, (piece_ref, back_ref) = refs[0:3], refs[3:6], refs[6:]
    for start in range(0, SENT, 160):
        rows = pl.ds(start, 160)
        x, c = xc_ref[rows, :WIDTH], xc_ref[rows, WIDTH:]
        total = None
        for gate_ref, up_ref, down_ref in (own, rest):
            act, slope, hidden = activate(x, gate_ref, up_ref)
            back_hidden = mm_last(c, down_ref[...])
            back_up = (back_hidden * act).astype(BF)
            back_gate = (back_hidden * slope).astype(BF)
            part = mm(back_gate, gate_ref[...]) + mm(back_up, up_ref[...])
            if total is None:
                back_ref[0, rows] = back_gate
                back_ref[1, rows] = back_up
                back_ref[2, rows] = hidden
                total = part
            else:
                total = total + part
        piece_ref[rows] = total.astype(BF)


def grads_body(*refs):
    hbm, out_hbm, vmem, (out_ref, bg2_ref, bu2_ref, hidden2_ref, sems) = refs[0:6], refs[6:10], refs[10:16], refs[16:]
    group = lax.axis_index("dp")
    chunks = [pl.ds(0, 160), pl.ds(160, 160)]
    rest_in = [pltpu.make_async_copy(hbm[0].at[r], vmem[0].at[r], sems.at[i]) for i, r in enumerate(chunks)]
    loads = [pltpu.make_async_copy(hbm[i], vmem[i], sems.at[1 + i]) for i in range(1, 6)]
    rest_ref, gate_ref, up_ref, down_ref, own_ref, back_ref = vmem
    for load in (rest_in[0], loads[0], loads[1], loads[2], rest_in[1]):
        load.start()
    for chunk, rows in enumerate(chunks):
        rest_in[chunk].wait()
        if chunk == 0:
            loads[0].wait()
            loads[1].wait()
        act, slope, hidden2_ref[rows] = activate(rest_ref[rows, :WIDTH], gate_ref, up_ref)
        if chunk == 0:
            loads[2].wait()
            loads[3].start()
            loads[4].start()
        back_hidden = mm_last(rest_ref[rows, WIDTH:], down_ref[...])
        bu2_ref[rows] = (back_hidden * act).astype(BF)
        bg2_ref[rows] = (back_hidden * slope).astype(BF)
    loads[3].wait()
    loads[4].wait()
    stores = []
    for kind, (lhs_rest, at) in enumerate(((bg2_ref, 0), (bu2_ref, 0), (hidden2_ref, WIDTH))):
        cols, rows = pl.ds(at, WIDTH), pl.ds(kind * HALF, HALF)
        total = mm_first(back_ref[kind], own_ref[:, cols]) + mm_first(lhs_rest[...], rest_ref[:, cols])
        out_ref[rows] = total.astype(BF)
        for shift in range(4):
            target = pl.ds(pl.multiple_of(((group + shift) & 3) * 256, 256), 256)
            copy = pltpu.make_async_copy(out_ref.at[rows, target], out_hbm[shift].at[rows], sems.at[7 + 4 * kind + shift])
            stores.append(copy)
            copy.start()
    for store in stores:
        store.wait()


def node_body(sel_ref, ret_ref, out_ref):
    out_ref[:, :WIDTH] = mm_first(sel_ref[:, :MSG], ret_ref[...]).astype(BF)
    out_ref[:, WIDTH:] = (
        mm_first(sel_ref[:, MSG : 2 * MSG], ret_ref[:, :MID])
        + mm_first(sel_ref[:, 2 * MSG :], ret_ref[:, MID:])
    ).astype(BF)


def early_body(*refs):
    total = refs[0][...].astype(F32)
    for ref in refs[1:-1]:
        total = total + ref[...].astype(F32)
    refs[-1][...] = total


def late_body(total_ref, *refs):
    for kind, out_ref in enumerate(refs[-3:]):
        part = pl.ds(kind * HALF, HALF)
        total = total_ref[part]
        for ref in refs[:-3]:
            total = total + ref[part].astype(F32)
        out_ref[...] = total.astype(BF)


def final_body(sel_ref, msg_ref, out_ref):
    low = msg_ref[:, WIDTH:]
    out_ref[:, :MID] = (mm_first(sel_ref[0], msg_ref[:, :MID]) + mm_first(sel_ref[1], low)).astype(BF)
    out_ref[:, MID:] = (mm_first(sel_ref[0], msg_ref[:, MID:WIDTH]) + mm_first(sel_ref[2], low)).astype(BF)


def call(body, ins, outs, flops, moved, *args, scratch=(), limit=60, dtype=BF):
    return pl.pallas_call(
        body,
        out_shape=tuple(jax.ShapeDtypeStruct(s, dtype) for s, _ in outs),
        in_specs=list(ins),
        out_specs=tuple(m for _, m in outs),
        scratch_shapes=list(scratch),
        compiler_params=pltpu.CompilerParams(vmem_limit_bytes=limit * 1024 * 1024),
        cost_estimate=pl.CostEstimate(flops=flops, bytes_accessed=moved, transcendentals=0),
        name=body.__name__,
    )(*args)


def over_nodes(x):
    return lax.all_to_all(x, "node", split_axis=0, concat_axis=0, tiled=True)


def over_chips(x):
    return lax.all_to_all(x, "local", split_axis=0, concat_axis=0, tiled=True, axis_index_groups=SAME_CORE)


def next_group(x, shift):
    return lax.ppermute(x, "dp", [(i, (i + shift) % 4) for i in range(4)])


def other_core(x):
    return lax.ppermute(x, "local", OTHER_CORE)


def on_device(tokens, upstream, expert_ids, gate_weights, w_gate, w_up, w_down):
    own = (w_gate[0], w_up[0], w_down[0])
    message, row_sel = call(
        route_body,
        [HBM] * 4,
        [((MSG, META + 128), VMEM), ((3, MSG, TOKS), HBM)],
        80_000_000,
        1_300_000,
        expert_ids.T,
        gate_weights.T,
        tokens,
        upstream,
        scratch=[
            pltpu.VMEM((4, TOKS), jnp.int32),
            pltpu.VMEM((4, TOKS), BF),
            pltpu.VMEM((TOKS, WIDTH), BF),
            pltpu.VMEM((TOKS, WIDTH), BF),
            pltpu.VMEM((3, MSG, TOKS), BF),
            pltpu.SemaphoreType.DMA((5,)),
        ],
    )
    message, *sent = lax.optimization_barrier((message, *own))
    arrived, *rest = lax.optimization_barrier((over_nodes(message), *(other_core(w) for w in sent)))
    placed, slot_sel = call(
        place_body,
        [VMEM],
        [((SENT, 2 * WIDTH), VMEM), ((SENT, 3 * MSG), HBM)],
        400_000_000,
        2_300_000,
        arrived,
        scratch=[pltpu.VMEM((SENT, 3 * MSG), BF), pltpu.VMEM((SENT, 3 * MSG), BF), pltpu.SemaphoreType.DMA],
        limit=16,
    )
    rows_own = over_chips(placed)
    rows_rest = other_core(rows_own)
    piece, back_own = call(
        own_body,
        [VMEM] * 7,
        [((SENT, WIDTH), VMEM), ((3, SENT, HALF), VMEM)],
        2_300_000_000,
        7_000_000,
        rows_own,
        *own,
        *rest,
        limit=24,
    )
    returned = over_chips(piece)
    grads = call(
        grads_body,
        [HBM] * 6,
        [((3 * HALF, 256), HBM)] * 4,
        2_100_000_000,
        8_000_000,
        rows_rest,
        *own,
        rows_own,
        back_own,
        scratch=[
            pltpu.VMEM((SENT, 2 * WIDTH), BF),
            *[pltpu.VMEM((HALF, WIDTH), BF)] * 3,
            pltpu.VMEM((SENT, 2 * WIDTH), BF),
            pltpu.VMEM((3, SENT, HALF), BF),
            pltpu.VMEM((3 * HALF, WIDTH), BF),
            *[pltpu.VMEM((SENT, HALF), BF)] * 3,
            pltpu.SemaphoreType.DMA((19,)),
        ],
    )
    returned, *grads = lax.optimization_barrier((returned, *grads))
    (node_sum,) = call(node_body, [VMEM] * 2, [((MSG, WIDE), VMEM)], 50_000_000_000, 1_300_000, slot_sel, returned, limit=16)
    (partial,) = call(
        early_body,
        [VMEM] * 2,
        [((3 * HALF, 256), VMEM)],
        50_000_000_000,
        2_700_000,
        grads[0],
        *(next_group(grads[shift], shift) for shift in (2,)),
        dtype=F32,
    )
    totals = call(
        late_body,
        [VMEM] * 3,
        [((HALF, 256), VMEM)] * 3,
        1_000_000,
        2_700_000,
        partial,
        *(next_group(grads[shift], shift) for shift in (1, 3)),
    )
    (token_grads,) = call(
        final_body,
        [VMEM] * 2,
        [((TOKS, WIDTH), VMEM)],
        50_000_000,
        700_000,
        row_sel,
        over_nodes(node_sum),
        limit=16,
    )
    return (token_grads, *[g[None] for g in totals])


def solution(mesh):
    tok = P(("dp", "node", "local"), None)
    weight = P(("node", "local"), None, None)
    grad = P(("node", "local"), None, "dp")
    return jax.shard_map(
        on_device,
        mesh=mesh,
        in_specs=(tok, tok, tok, tok, weight, weight, weight),
        out_specs=(tok, grad, grad, grad),
        check_vma=False,
    )
```

```python
import jax
import jax.numpy as jnp
from jax import lax
from jax.experimental import pallas as pl
from jax.experimental.pallas import tpu as pltpu
from jax.sharding import PartitionSpec as P

WIDTH = 1024
MID = 512
WIDE = 1536
META = 3072
HALF = 352
TOKS = 64
MSG = 128
CAP = 5
STEP = 320
SLOT = 80
SENT = 320
F32 = jnp.float32
BF = jnp.bfloat16
SAME_CORE = [[0, 2, 4, 6], [1, 3, 5, 7]]
OTHER_CORE = [(i, i ^ 1) for i in range(8)]
VMEM = pl.BlockSpec(memory_space=pltpu.VMEM)
HBM = pl.BlockSpec(memory_space=pltpu.HBM)


def mm(a, b):
    return jnp.dot(a, b, preferred_element_type=F32)


def mm_first(a, b):
    return lax.dot_general(a, b, (((0,), (0,)), ((), ())), preferred_element_type=F32)


def mm_last(a, b):
    return lax.dot_general(a, b, (((1,), (1,)), ((), ())), preferred_element_type=F32)


def iota(shape, dim):
    return lax.broadcasted_iota(jnp.int32, shape, dim)


def one(cond):
    return jnp.where(cond, 1.0, 0.0).astype(BF)


def route_body(ids_hbm, gate_hbm, tok_hbm, up_hbm, msg_hbm, sel_hbm, ids_ref, gate_ref, tok_ref, up_ref, msg_ref, sel_ref, sems):
    pairs = ((ids_hbm, ids_ref), (gate_hbm, gate_ref), (tok_hbm, tok_ref), (up_hbm, up_ref))
    loads = [pltpu.make_async_copy(src, dst, sems.at[i]) for i, (src, dst) in enumerate(pairs)]
    for load in loads:
        load.start()
    loads[0].wait()
    loads[1].wait()
    ids = ids_ref[...]
    gates = gate_ref[...].astype(F32)
    node = iota((MSG, TOKS), 0) >> 3
    expert = iota((TOKS, TOKS), 0)
    named = jnp.zeros((MSG, TOKS), F32)
    weight = jnp.zeros((TOKS, TOKS), F32)
    for k in range(4):
        row = ids[k : k + 1]
        named = jnp.where((row >> 2) == node, 1.0, named)
        weight = jnp.where(row == expert, gates[k : k + 1], weight)
    weight = weight.astype(BF)
    hit = named > 0.5
    rank = mm(named.astype(BF), one(iota((TOKS, TOKS), 0) < iota((TOKS, TOKS), 1))).astype(jnp.int32)
    place = iota((MSG, TOKS), 0) & 7
    late = hit & (rank == 8 + (place & 3))
    whole = one(hit & (rank == place))
    left = one(late & (place < 4))
    right = one(late & (place >= 4))
    sel_ref[0] = whole
    sel_ref[1] = left
    sel_ref[2] = right
    stores = [pltpu.make_async_copy(sel_ref, sel_hbm, sems.at[4])]
    stores[0].start()
    own_node = (iota((MSG, TOKS), 1) >> 2) == node
    gate_whole = jnp.where(own_node, mm_last(whole, weight), 0.0).astype(BF)
    gate_late = jnp.where(own_node, mm_last(left + right, weight), 0.0).astype(BF)
    fold_row, fold_col = iota((TOKS, MSG), 0) & 3, iota((TOKS, MSG), 1)
    meta = mm(gate_whole, one(fold_col == fold_row)) + mm(gate_late, one(fold_col == fold_row + 8))
    msg_ref[:, META:] = meta.astype(BF)
    for load, src, base in ((loads[2], tok_ref, 0), (loads[3], up_ref, WIDE)):
        load.wait()
        msg_ref[:, base : base + WIDTH] = mm(whole, src[...]).astype(BF)
        low = mm(left, src[:, :MID]) + mm(right, src[:, MID:])
        msg_ref[:, base + WIDTH : base + WIDE] = low.astype(BF)
        part = pl.ds(base, WIDE + base // 12)
        stores.append(pltpu.make_async_copy(msg_ref.at[:, part], msg_hbm.at[:, part], sems.at[5 + len(stores)]))
        stores[-1].start()
    for store in stores:
        store.wait()


def spread(sel, msg_ref, at, out_ref, to):
    low = msg_ref[:, at + WIDTH : at + WIDE]
    left = mm(sel[:, :MSG], msg_ref[:, at : at + MID]) + mm(sel[:, MSG : 2 * MSG], low)
    right = mm(sel[:, :MSG], msg_ref[:, at + MID : at + WIDTH]) + mm(sel[:, 2 * MSG :], low)
    out_ref[:, to : to + MID] = left.astype(BF)
    out_ref[:, to + MID : to + WIDTH] = right.astype(BF)


def fill(slot, sel_ref, part, gate=None):
    slots = iota((SLOT, MSG), 0).astype(slot.dtype)
    for j in range(4):
        value = 1.0 if gate is None else gate[j : j + 1]
        match = jnp.where(slots == slot[j : j + 1], value, 0.0)
        sel_ref[pl.ds(j * SLOT, SLOT), pl.ds(part * MSG, MSG)] = match.astype(BF)


def place_body(msg_ref, out_ref, slot_ref, sel_ref, gated_ref):
    row, col = iota((MSG, MSG), 0), iota((MSG, MSG), 1)
    gates = mm_first(msg_ref[:, META:], one(row == col))
    gate_whole, gate_late = gates[0:8], gates[8:16]
    has_whole, has_late = one(gate_whole > 0.0), one(gate_late > 0.0)
    same = (row >> 3) == (col >> 3)
    rank_whole = mm(has_whole, one(same & (row < col)))
    rank_late = mm(has_whole, one(same)) + mm(has_late, one(same & ((row & 7) < (col & 3))))
    node = (iota((8, MSG), 1) >> 3) * CAP
    lane_place = iota((8, MSG), 1) & 7
    slot_whole = jnp.where(gate_whole > 0.0, node + rank_whole.astype(jnp.int32), -1)
    slot_late = jnp.where(gate_late > 0.0, node + rank_late.astype(jnp.int32), -1)
    slot_left = jnp.where(lane_place < 4, slot_late, -1)
    slot_right = jnp.where(lane_place >= 4, slot_late, -1)
    for part, (slot, gate) in enumerate(((slot_whole, gate_whole), (slot_left, gate_late), (slot_right, gate_late))):
        slot_ref[16 * part : 16 * part + 16] = jnp.concatenate([slot, slot], 0).astype(F32).astype(BF)
        fill(slot, sel_ref, part)
        fill(slot, gated_ref, part, gate)
    spread(sel_ref, msg_ref, 0, out_ref, 0)
    spread(gated_ref, msg_ref, WIDE, out_ref, WIDTH)


def activate(x, gate_ref, up_ref):
    gate_logit = mm_last(x, gate_ref[...])
    up_value = mm_last(x, up_ref[...])
    sig = jax.nn.sigmoid(gate_logit)
    act = gate_logit * sig
    return act, up_value * sig * (1.0 + gate_logit * (1.0 - sig)), (act * up_value).astype(BF)


def own_body(xc_ref, *refs):
    own, rest, piece_ref = refs[0:3], refs[3:6], refs[6]
    for start in range(0, SENT, STEP):
        rows = pl.ds(start, STEP)
        x, c = xc_ref[rows, :WIDTH], xc_ref[rows, WIDTH:]
        total = None
        for gate_ref, up_ref, down_ref in (own, rest):
            act, slope, _ = activate(x, gate_ref, up_ref)
            back_hidden = mm_last(c, down_ref[...])
            back_up = (back_hidden * act).astype(BF)
            back_gate = (back_hidden * slope).astype(BF)
            part = mm(back_gate, gate_ref[...]) + mm(back_up, up_ref[...])
            total = part if total is None else total + part
        piece_ref[rows] = total.astype(BF)


def grads_body(*refs):
    hbm, out_hbm, vmem, (out_ref, sems) = refs[0:5], refs[5:9], refs[9:14], refs[14:]
    group = lax.axis_index("dp")
    own_ref, gate_ref, up_ref, down_ref, rest_ref = vmem
    loads = [pltpu.make_async_copy(src, dst, sems.at[i]) for i, (src, dst) in enumerate(zip(hbm, vmem))]
    for load in loads[:4]:
        load.start()
    for load in loads[:3]:
        load.wait()
    loads[4].start()
    backs = []
    for rows_ref, ready in ((own_ref, loads[3]), (rest_ref, loads[4])):
        if rows_ref is rest_ref:
            ready.wait()
        x = rows_ref[:, :WIDTH]
        gate_logit, up_value = mm_last(gate_ref[...], x), mm_last(up_ref[...], x)
        sig = jax.nn.sigmoid(gate_logit)
        act = gate_logit * sig
        if rows_ref is own_ref:
            ready.wait()
        back_hidden = mm_last(down_ref[...], rows_ref[:, WIDTH:])
        slope = up_value * sig * (1.0 + gate_logit * (1.0 - sig))
        backs.append([(back_hidden * slope).astype(BF), (back_hidden * act).astype(BF), (act * up_value).astype(BF)])
    stores = []
    for kind, at in enumerate((0, 0, WIDTH)):
        cols, rows = pl.ds(at, WIDTH), pl.ds(kind * HALF, HALF)
        total = mm(backs[0][kind], own_ref[:, cols]) + mm(backs[1][kind], rest_ref[:, cols])
        out_ref[rows] = total.astype(BF)
        for shift in range(4):
            target = pl.ds(pl.multiple_of(((group + shift) & 3) * 256, 256), 256)
            copy = pltpu.make_async_copy(out_ref.at[rows, target], out_hbm[shift].at[rows], sems.at[5 + 4 * kind + shift])
            stores.append(copy)
            copy.start()
    for store in stores:
        store.wait()


def node_body(slot_ref, ret_ref, out_ref, sel_ref):
    for part in range(3):
        fill(slot_ref[16 * part : 16 * part + 16].astype(F32), sel_ref, part)
    out_ref[:, :WIDTH] = mm_first(sel_ref[:, :MSG], ret_ref[...]).astype(BF)
    out_ref[:, WIDTH:] = (
        mm_first(sel_ref[:, MSG : 2 * MSG], ret_ref[:, :MID])
        + mm_first(sel_ref[:, 2 * MSG :], ret_ref[:, MID:])
    ).astype(BF)


def early_body(*refs):
    total = refs[0][...].astype(F32)
    for ref in refs[1:-1]:
        total = total + ref[...].astype(F32)
    refs[-1][...] = total


def late_body(total_ref, *refs):
    for kind, out_ref in enumerate(refs[-3:]):
        part = pl.ds(kind * HALF, HALF)
        total = total_ref[part]
        for ref in refs[:-3]:
            total = total + ref[part].astype(F32)
        out_ref[...] = total.astype(BF)


def final_body(sel_ref, msg_ref, out_ref):
    low = msg_ref[:, WIDTH:]
    out_ref[:, :MID] = (mm_first(sel_ref[0], msg_ref[:, :MID]) + mm_first(sel_ref[1], low)).astype(BF)
    out_ref[:, MID:] = (mm_first(sel_ref[0], msg_ref[:, MID:WIDTH]) + mm_first(sel_ref[2], low)).astype(BF)


def call(body, ins, outs, flops, moved, *args, scratch=(), limit=60, dtype=BF):
    return pl.pallas_call(
        body,
        out_shape=tuple(jax.ShapeDtypeStruct(s, dtype) for s, _ in outs),
        in_specs=list(ins),
        out_specs=tuple(m for _, m in outs),
        scratch_shapes=list(scratch),
        compiler_params=pltpu.CompilerParams(vmem_limit_bytes=limit * 1024 * 1024),
        cost_estimate=pl.CostEstimate(flops=flops, bytes_accessed=moved, transcendentals=0),
        name=body.__name__,
    )(*args)


def over_nodes(x):
    return lax.all_to_all(x, "node", split_axis=0, concat_axis=0, tiled=True)


def over_chips(x):
    return lax.all_to_all(x, "local", split_axis=0, concat_axis=0, tiled=True, axis_index_groups=SAME_CORE)


def next_group(x, shift):
    return lax.ppermute(x, "dp", [(i, (i + shift) % 4) for i in range(4)])


def other_core(x):
    return lax.ppermute(x, "local", OTHER_CORE)


def on_device(tokens, upstream, expert_ids, gate_weights, w_gate, w_up, w_down):
    own = (w_gate[0], w_up[0], w_down[0])
    message, row_sel = call(
        route_body,
        [HBM] * 4,
        [((MSG, META + 128), HBM), ((3, MSG, TOKS), HBM)],
        80_000_000,
        1_300_000,
        expert_ids.T,
        gate_weights.T,
        tokens,
        upstream,
        scratch=[
            pltpu.VMEM((4, TOKS), jnp.int32),
            pltpu.VMEM((4, TOKS), BF),
            pltpu.VMEM((TOKS, WIDTH), BF),
            pltpu.VMEM((TOKS, WIDTH), BF),
            pltpu.VMEM((MSG, META + 128), BF),
            pltpu.VMEM((3, MSG, TOKS), BF),
            pltpu.SemaphoreType.DMA((8,)),
        ],
    )
    message, *sent = lax.optimization_barrier((message, *own))
    arrived, *rest = lax.optimization_barrier((over_nodes(message), *(other_core(w) for w in sent)))
    placed, node_slots = call(
        place_body,
        [VMEM],
        [((SENT, 2 * WIDTH), VMEM), ((48, MSG), VMEM)],
        400_000_000,
        2_300_000,
        arrived,
        scratch=[pltpu.VMEM((SENT, 3 * MSG), BF)] * 2,
        limit=16,
    )
    rows_own = over_chips(placed)
    (piece,) = call(
        own_body,
        [VMEM] * 7,
        [((SENT, WIDTH), VMEM)],
        2_300_000_000,
        7_000_000,
        rows_own,
        *own,
        *rest,
        limit=24,
    )
    piece, rows_sent = lax.optimization_barrier((piece, rows_own))
    rows_rest = other_core(rows_sent)
    returned = over_chips(piece)
    grads = call(
        grads_body,
        [HBM] * 5,
        [((3 * HALF, 256), HBM)] * 4,
        2_800_000_000,
        8_000_000,
        rows_own,
        *own,
        rows_rest,
        scratch=[
            pltpu.VMEM((SENT, 2 * WIDTH), BF),
            *[pltpu.VMEM((HALF, WIDTH), BF)] * 3,
            pltpu.VMEM((SENT, 2 * WIDTH), BF),
            pltpu.VMEM((3 * HALF, WIDTH), BF),
            pltpu.SemaphoreType.DMA((17,)),
        ],
    )
    returned, *grads = lax.optimization_barrier((returned, *grads))
    (node_sum,) = call(
        node_body,
        [VMEM] * 2,
        [((MSG, WIDE), VMEM)],
        50_000_000_000,
        1_300_000,
        node_slots,
        returned,
        scratch=[pltpu.VMEM((SENT, 3 * MSG), BF)],
        limit=16,
    )
    (partial,) = call(
        early_body,
        [VMEM] * 2,
        [((3 * HALF, 256), VMEM)],
        50_000_000_000,
        2_700_000,
        grads[0],
        *(next_group(grads[shift], shift) for shift in (2,)),
        dtype=F32,
        limit=24,
    )
    totals = call(
        late_body,
        [VMEM] * 3,
        [((HALF, 256), VMEM)] * 3,
        1_000_000,
        2_700_000,
        partial,
        *(next_group(grads[shift], shift) for shift in (1, 3)),
        limit=24,
    )
    (token_grads,) = call(
        final_body,
        [VMEM] * 2,
        [((TOKS, WIDTH), VMEM)],
        50_000_000,
        700_000,
        row_sel,
        over_nodes(node_sum),
        limit=16,
    )
    return (token_grads, *[g[None] for g in totals])


def solution(mesh):
    tok = P(("dp", "node", "local"), None)
    weight = P(("node", "local"), None, None)
    grad = P(("node", "local"), None, "dp")
    return jax.shard_map(
        on_device,
        mesh=mesh,
        in_specs=(tok, tok, tok, tok, weight, weight, weight),
        out_specs=(tok, grad, grad, grad),
        check_vma=False,
    )
```

```python
import jax
import jax.numpy as jnp
from jax import lax
from jax.experimental import pallas as pl
from jax.experimental.pallas import tpu as pltpu
from jax.sharding import PartitionSpec as P

WIDTH = 1024
MID = 512
WIDE = 1536
META = 3072
HALF = 352
TOKS = 64
MSG = 128
CAP = 5
STEP = 320
SLOT = 80
SENT = 320
F32 = jnp.float32
BF = jnp.bfloat16
SAME_CORE = [[0, 2, 4, 6], [1, 3, 5, 7]]
OTHER_CORE = [(i, i ^ 1) for i in range(8)]
VMEM = pl.BlockSpec(memory_space=pltpu.VMEM)
HBM = pl.BlockSpec(memory_space=pltpu.HBM)


def mm(a, b):
    return jnp.dot(a, b, preferred_element_type=F32)


def mm_first(a, b):
    return lax.dot_general(a, b, (((0,), (0,)), ((), ())), preferred_element_type=F32)


def mm_last(a, b):
    return lax.dot_general(a, b, (((1,), (1,)), ((), ())), preferred_element_type=F32)


def iota(shape, dim):
    return lax.broadcasted_iota(jnp.int32, shape, dim)


def one(cond):
    return jnp.where(cond, 1.0, 0.0).astype(BF)


def route_body(ids_hbm, gate_hbm, tok_hbm, up_hbm, msg_hbm, sel_hbm, ids_ref, gate_ref, tok_ref, up_ref, msg_ref, sel_ref, sems):
    pairs = ((ids_hbm, ids_ref), (gate_hbm, gate_ref), (tok_hbm, tok_ref), (up_hbm, up_ref))
    loads = [pltpu.make_async_copy(src, dst, sems.at[i]) for i, (src, dst) in enumerate(pairs)]
    for load in loads:
        load.start()
    loads[0].wait()
    loads[1].wait()
    ids = ids_ref[...]
    gates = gate_ref[...].astype(F32)
    node = iota((MSG, TOKS), 0) >> 3
    expert = iota((TOKS, TOKS), 0)
    named = jnp.zeros((MSG, TOKS), F32)
    weight = jnp.zeros((TOKS, TOKS), F32)
    for k in range(4):
        row = ids[k : k + 1]
        named = jnp.where((row >> 2) == node, 1.0, named)
        weight = jnp.where(row == expert, gates[k : k + 1], weight)
    weight = weight.astype(BF)
    hit = named > 0.5
    rank = mm(named.astype(BF), one(iota((TOKS, TOKS), 0) < iota((TOKS, TOKS), 1))).astype(jnp.int32)
    place = iota((MSG, TOKS), 0) & 7
    late = hit & (rank == 8 + (place & 3))
    whole = one(hit & (rank == place))
    left = one(late & (place < 4))
    right = one(late & (place >= 4))
    sel_ref[0] = whole
    sel_ref[1] = left
    sel_ref[2] = right
    stores = [pltpu.make_async_copy(sel_ref, sel_hbm, sems.at[4])]
    stores[0].start()
    own_node = (iota((MSG, TOKS), 1) >> 2) == node
    gate_whole = jnp.where(own_node, mm_last(whole, weight), 0.0).astype(BF)
    gate_late = jnp.where(own_node, mm_last(left + right, weight), 0.0).astype(BF)
    fold_row, fold_col = iota((TOKS, MSG), 0) & 3, iota((TOKS, MSG), 1)
    meta = mm(gate_whole, one(fold_col == fold_row)) + mm(gate_late, one(fold_col == fold_row + 8))
    msg_ref[:, META:] = meta.astype(BF)
    for load, src, base in ((loads[2], tok_ref, 0), (loads[3], up_ref, WIDE)):
        load.wait()
        msg_ref[:, base : base + WIDTH] = mm(whole, src[...]).astype(BF)
        low = mm(left, src[:, :MID]) + mm(right, src[:, MID:])
        msg_ref[:, base + WIDTH : base + WIDE] = low.astype(BF)
        part = pl.ds(base, WIDE + base // 12)
        stores.append(pltpu.make_async_copy(msg_ref.at[:, part], msg_hbm.at[:, part], sems.at[5 + len(stores)]))
        stores[-1].start()
    for store in stores:
        store.wait()


def spread(sel, msg_ref, at, out_ref, to):
    low = msg_ref[:, at + WIDTH : at + WIDE]
    left = mm(sel[:, :MSG], msg_ref[:, at : at + MID]) + mm(sel[:, MSG : 2 * MSG], low)
    right = mm(sel[:, :MSG], msg_ref[:, at + MID : at + WIDTH]) + mm(sel[:, 2 * MSG :], low)
    out_ref[:, to : to + MID] = left.astype(BF)
    out_ref[:, to + MID : to + WIDTH] = right.astype(BF)


def fill(slot, sel_ref, part, gate=None):
    slots = iota((SLOT, MSG), 0).astype(slot.dtype)
    for j in range(4):
        value = 1.0 if gate is None else gate[j : j + 1]
        match = jnp.where(slots == slot[j : j + 1], value, 0.0)
        sel_ref[pl.ds(j * SLOT, SLOT), pl.ds(part * MSG, MSG)] = match.astype(BF)


def place_body(msg_ref, out_ref, slot_ref, sel_ref, gated_ref):
    row, col = iota((MSG, MSG), 0), iota((MSG, MSG), 1)
    gates = mm_first(msg_ref[:, META:], one(row == col))
    gate_whole, gate_late = gates[0:8], gates[8:16]
    has_whole, has_late = one(gate_whole > 0.0), one(gate_late > 0.0)
    same = (row >> 3) == (col >> 3)
    rank_whole = mm(has_whole, one(same & (row < col)))
    rank_late = mm(has_whole, one(same)) + mm(has_late, one(same & ((row & 7) < (col & 3))))
    node = (iota((8, MSG), 1) >> 3) * CAP
    lane_place = iota((8, MSG), 1) & 7
    slot_whole = jnp.where(gate_whole > 0.0, node + rank_whole.astype(jnp.int32), -1)
    slot_late = jnp.where(gate_late > 0.0, node + rank_late.astype(jnp.int32), -1)
    slot_left = jnp.where(lane_place < 4, slot_late, -1)
    slot_right = jnp.where(lane_place >= 4, slot_late, -1)
    for part, (slot, gate) in enumerate(((slot_whole, gate_whole), (slot_left, gate_late), (slot_right, gate_late))):
        slot_ref[16 * part : 16 * part + 16] = jnp.concatenate([slot, slot], 0).astype(F32).astype(BF)
        fill(slot, sel_ref, part)
        fill(slot, gated_ref, part, gate)
    spread(sel_ref, msg_ref, 0, out_ref, 0)
    spread(gated_ref, msg_ref, WIDE, out_ref, WIDTH)


def activate(x, gate_ref, up_ref):
    gate_logit = mm_last(x, gate_ref[...])
    up_value = mm_last(x, up_ref[...])
    sig = jax.nn.sigmoid(gate_logit)
    act = gate_logit * sig
    return act, up_value * sig * (1.0 + gate_logit * (1.0 - sig)), (act * up_value).astype(BF)


def own_body(xc_ref, *refs):
    own, rest, piece_ref = refs[0:3], refs[3:6], refs[6]
    for start in range(0, SENT, STEP):
        rows = pl.ds(start, STEP)
        x, c = xc_ref[rows, :WIDTH], xc_ref[rows, WIDTH:]
        total = None
        for gate_ref, up_ref, down_ref in (own, rest):
            act, slope, _ = activate(x, gate_ref, up_ref)
            back_hidden = mm_last(c, down_ref[...])
            back_up = (back_hidden * act).astype(BF)
            back_gate = (back_hidden * slope).astype(BF)
            part = mm(back_gate, gate_ref[...]) + mm(back_up, up_ref[...])
            total = part if total is None else total + part
        piece_ref[rows] = total.astype(BF)


def grads_body(*refs):
    hbm, out_hbm, vmem, (out_ref, sems) = refs[0:5], refs[5:9], refs[9:14], refs[14:]
    group = lax.axis_index("dp")
    own_ref, gate_ref, up_ref, down_ref, rest_ref = vmem
    halves = (pl.ds(0, WIDTH), pl.ds(WIDTH, WIDTH))
    weights = [pltpu.make_async_copy(hbm[i], vmem[i], sems.at[i]) for i in (1, 2, 3)]
    own_in, rest_in = [
        [pltpu.make_async_copy(hbm[i].at[:, cols], vmem[i].at[:, cols], sems.at[at + k]) for k, cols in enumerate(halves)]
        for i, at in ((0, 17), (4, 19))
    ]
    for load in (own_in[0], weights[0], weights[1]):
        load.start()
    backs = []
    for rows_ref, loads in ((own_ref, own_in), (rest_ref, rest_in)):
        first = rows_ref is own_ref
        loads[0].wait()
        if first:
            weights[0].wait()
            for load in (own_in[1], weights[2], *rest_in):
                load.start()
        x = rows_ref[:, :WIDTH]
        gate_logit = mm_last(gate_ref[...], x)
        if first:
            weights[1].wait()
        up_value = mm_last(up_ref[...], x)
        sig = jax.nn.sigmoid(gate_logit)
        act = gate_logit * sig
        loads[1].wait()
        if first:
            weights[2].wait()
        back_hidden = mm_last(down_ref[...], rows_ref[:, WIDTH:])
        slope = up_value * sig * (1.0 + gate_logit * (1.0 - sig))
        backs.append([(back_hidden * slope).astype(BF), (back_hidden * act).astype(BF), (act * up_value).astype(BF)])
    stores = []
    for kind, at in enumerate((0, 0, WIDTH)):
        cols, rows = pl.ds(at, WIDTH), pl.ds(kind * HALF, HALF)
        total = mm(backs[0][kind], own_ref[:, cols]) + mm(backs[1][kind], rest_ref[:, cols])
        out_ref[rows] = total.astype(BF)
        for shift in range(4):
            target = pl.ds(pl.multiple_of(((group + shift) & 3) * 256, 256), 256)
            copy = pltpu.make_async_copy(out_ref.at[rows, target], out_hbm[shift].at[rows], sems.at[5 + 4 * kind + shift])
            stores.append(copy)
            copy.start()
    for store in stores:
        store.wait()


def node_body(slot_ref, ret_ref, out_ref, sel_ref):
    for part in range(3):
        fill(slot_ref[16 * part : 16 * part + 16].astype(F32), sel_ref, part)
    out_ref[:, :WIDTH] = mm_first(sel_ref[:, :MSG], ret_ref[...]).astype(BF)
    out_ref[:, WIDTH:] = (
        mm_first(sel_ref[:, MSG : 2 * MSG], ret_ref[:, :MID])
        + mm_first(sel_ref[:, 2 * MSG :], ret_ref[:, MID:])
    ).astype(BF)


def early_body(*refs):
    total = refs[0][...].astype(F32)
    for ref in refs[1:-1]:
        total = total + ref[...].astype(F32)
    refs[-1][...] = total


def late_body(total_ref, *refs):
    for kind, out_ref in enumerate(refs[-3:]):
        part = pl.ds(kind * HALF, HALF)
        total = total_ref[part]
        for ref in refs[:-3]:
            total = total + ref[part].astype(F32)
        out_ref[...] = total.astype(BF)


def final_body(sel_ref, msg_ref, out_ref):
    low = msg_ref[:, WIDTH:]
    out_ref[:, :MID] = (mm_first(sel_ref[0], msg_ref[:, :MID]) + mm_first(sel_ref[1], low)).astype(BF)
    out_ref[:, MID:] = (mm_first(sel_ref[0], msg_ref[:, MID:WIDTH]) + mm_first(sel_ref[2], low)).astype(BF)


def call(body, ins, outs, flops, moved, *args, scratch=(), limit=60, dtype=BF):
    return pl.pallas_call(
        body,
        out_shape=tuple(jax.ShapeDtypeStruct(s, dtype) for s, _ in outs),
        in_specs=list(ins),
        out_specs=tuple(m for _, m in outs),
        scratch_shapes=list(scratch),
        compiler_params=pltpu.CompilerParams(vmem_limit_bytes=limit * 1024 * 1024),
        cost_estimate=pl.CostEstimate(flops=flops, bytes_accessed=moved, transcendentals=0),
        name=body.__name__,
    )(*args)


def over_nodes(x):
    return lax.all_to_all(x, "node", split_axis=0, concat_axis=0, tiled=True)


def over_chips(x):
    return lax.all_to_all(x, "local", split_axis=0, concat_axis=0, tiled=True, axis_index_groups=SAME_CORE)


def next_group(x, shift):
    return lax.ppermute(x, "dp", [(i, (i + shift) % 4) for i in range(4)])


def other_core(x):
    return lax.ppermute(x, "local", OTHER_CORE)


def on_device(tokens, upstream, expert_ids, gate_weights, w_gate, w_up, w_down):
    own = (w_gate[0], w_up[0], w_down[0])
    message, row_sel = call(
        route_body,
        [HBM] * 4,
        [((MSG, META + 128), HBM), ((3, MSG, TOKS), HBM)],
        80_000_000,
        1_300_000,
        expert_ids.T,
        gate_weights.T,
        tokens,
        upstream,
        scratch=[
            pltpu.VMEM((4, TOKS), jnp.int32),
            pltpu.VMEM((4, TOKS), BF),
            pltpu.VMEM((TOKS, WIDTH), BF),
            pltpu.VMEM((TOKS, WIDTH), BF),
            pltpu.VMEM((MSG, META + 128), BF),
            pltpu.VMEM((3, MSG, TOKS), BF),
            pltpu.SemaphoreType.DMA((8,)),
        ],
    )
    message, *sent = lax.optimization_barrier((message, *own))
    arrived, *rest = lax.optimization_barrier((over_nodes(message), *(other_core(w) for w in sent)))
    placed, node_slots = call(
        place_body,
        [VMEM],
        [((SENT, 2 * WIDTH), VMEM), ((48, MSG), VMEM)],
        400_000_000,
        2_300_000,
        arrived,
        scratch=[pltpu.VMEM((SENT, 3 * MSG), BF)] * 2,
        limit=16,
    )
    rows_own = over_chips(placed)
    (piece,) = call(
        own_body,
        [VMEM] * 7,
        [((SENT, WIDTH), VMEM)],
        2_300_000_000,
        7_000_000,
        rows_own,
        *own,
        *rest,
        limit=24,
    )
    rows_rest = other_core(rows_own)
    returned = over_chips(piece)
    grads = call(
        grads_body,
        [HBM] * 5,
        [((3 * HALF, 256), HBM)] * 4,
        2_800_000_000,
        8_000_000,
        rows_own,
        *own,
        rows_rest,
        scratch=[
            pltpu.VMEM((SENT, 2 * WIDTH), BF),
            *[pltpu.VMEM((HALF, WIDTH), BF)] * 3,
            pltpu.VMEM((SENT, 2 * WIDTH), BF),
            pltpu.VMEM((3 * HALF, WIDTH), BF),
            pltpu.SemaphoreType.DMA((21,)),
        ],
    )
    returned, *grads = lax.optimization_barrier((returned, *grads))
    (node_sum,) = call(
        node_body,
        [VMEM] * 2,
        [((MSG, WIDE), VMEM)],
        50_000_000_000,
        1_300_000,
        node_slots,
        returned,
        scratch=[pltpu.VMEM((SENT, 3 * MSG), BF)],
        limit=16,
    )
    (partial,) = call(
        early_body,
        [VMEM] * 2,
        [((3 * HALF, 256), VMEM)],
        50_000_000_000,
        2_700_000,
        grads[0],
        *(next_group(grads[shift], shift) for shift in (2,)),
        dtype=F32,
        limit=24,
    )
    totals = call(
        late_body,
        [VMEM] * 3,
        [((HALF, 256), VMEM)] * 3,
        1_000_000,
        2_700_000,
        partial,
        *(next_group(grads[shift], shift) for shift in (1, 3)),
        limit=24,
    )
    (token_grads,) = call(
        final_body,
        [VMEM] * 2,
        [((TOKS, WIDTH), VMEM)],
        50_000_000,
        700_000,
        row_sel,
        over_nodes(node_sum),
        limit=16,
    )
    return (token_grads, *[g[None] for g in totals])


def solution(mesh):
    tok = P(("dp", "node", "local"), None)
    weight = P(("node", "local"), None, None)
    grad = P(("node", "local"), None, "dp")
    return jax.shard_map(
        on_device,
        mesh=mesh,
        in_specs=(tok, tok, tok, tok, weight, weight, weight),
        out_specs=(tok, grad, grad, grad),
        check_vma=False,
    )
```
